512 devices in a mesh: mp: 16 (over y, z_hi), shard: 32 (over x, z_lo, core).
Axes of the slice: x: 4, y: 4, z: 16 (z_hi: 4, z_lo: 4; z = z_hi * 4 + z_lo), core: 2. Of those that a mesh axis runs over, the one named last changes fastest.
Arguments:
- activations: bfloat16 [16, 128, 14336], P('mp', 'shard'), may hold values from -6 to 6
- out_grads: bfloat16 [16, 128, 4096], P('mp', 'shard'), may hold values from -0.3984375 to 0.3984375
- owners: int32 [16, 128], P('mp', 'shard'), may hold values from 0 to 1, never falling along the last dimension, each value on 1 to 96 neighbouring positions
- weights: bfloat16 [16, 14336, 4096], P('mp', 'shard'), may hold values from -6 to 6
Outputs:
- merged: bfloat16 [14336, 4096], P('shard', 'mp')
The draws below stay inside these ranges and needn't reach their ends.
Inputs may be any that keep to these rules, and one draw needn't show every extreme that they name: owners gives each token's sequence; each sequence of a model is one contiguous run of 1 to 96 tokens, in increasing order of sequence.
All inputs are finite; a program needn't handle non-finite values.
Results may differ from the reference program's by a relative error of at most 0.0045.
Values may be sent and summed in bfloat16 or wider, within the bound.
A program may use at most 128 MiB of HBM per device.

```python
import math
import jax
import jax.numpy as jnp
import numpy as np
from jax import lax

D = 4096
FF = 14336
NSEQ = 2
MODELS = 16
TOKENS = 128
LONGEST = 96


def level_of(rng, extent, cuts, smallest, top_value):
    loudness, own = 1.0, jax.random.fold_in(rng, 6)
    for axis_at, blocks in cuts:
        draws = jnp.exp(jax.random.uniform(jax.random.fold_in(own, axis_at), (blocks,), jnp.float32, smallest / len(cuts), top_value / len(cuts)))
        loudness = loudness * jnp.repeat(draws, extent[axis_at] // blocks).reshape([-1 if axis == axis_at else 1 for axis in range(len(extent))])
    return loudness


def split_up(amount, total, most, skew):
    portions = [(1 << 20) // math.isqrt(grade ** skew) + 1 for grade in range(2, amount + 1)]
    surplus, holding = total - most - (amount - 1), [1] * (amount - 1)
    while surplus > 0:
        movable = [i for i in range(amount - 1) if holding[i] < most]
        pool, remaining = sum([portions[i] for i in movable]), surplus
        for i in movable:
            extra = min(most - holding[i], max(1, remaining * portions[i] // pool), surplus)
            holding[i] = holding[i] + extra
            surplus = surplus - extra
    return np.array([most] + holding)


def uneven(rng, count, total, limit, lean):
    if count == 2:
        one = jax.random.randint(rng, (), max(1, total - limit), min(limit, total - 1) + 1)
        return jnp.stack([one, total - one])
    tallies = jnp.asarray(split_up(count, total, limit, lean), jnp.int32)
    twos = (count - 1) // 2
    donor, receiver = tallies[1:1 + 2 * twos:2], tallies[2:2 + 2 * twos:2]
    room = jnp.minimum(donor - 1, limit - receiver)
    shifted = jax.random.randint(jax.random.fold_in(rng, 1), (twos,), 0, 1 << 20) % (room + 1)
    tallies = tallies.at[1:1 + 2 * twos:2].set(donor - shifted).at[2:2 + 2 * twos:2].set(receiver + shifted)
    return tallies[jax.random.permutation(jax.random.fold_in(rng, 2), count)]


def scatter_about(stream_key, extent, deviation, reach, cuts=(), dtype=jnp.bfloat16):
    gain = level_of(stream_key, extent, cuts, -0.22, 0.18) if cuts else 1.0
    drawn = jax.random.normal(stream_key, extent, jnp.float32) * deviation * gain
    return jnp.minimum(jnp.maximum(drawn, -reach), reach).astype(dtype)


def setup_inputs(seed: int = 0) -> dict:
    splits = jax.random.split(jax.random.key(seed), 5)
    activations = scatter_about(splits[0], (MODELS, TOKENS, FF), 1.0, 6.0, ((0, 16), (1, 32)))
    out_grads = scatter_about(splits[1], (MODELS, TOKENS, D), 0.0625, 0.3984375, ((0, 16), (1, 32)))
    owners = jax.vmap(lambda own: jnp.searchsorted(jnp.cumsum(uneven(own, NSEQ, TOKENS, LONGEST, 2)), jnp.arange(TOKENS), side="right"))(jax.random.split(splits[2], MODELS)).reshape((MODELS, TOKENS)).astype(jnp.int32)
    weights = scatter_about(splits[3], (MODELS, FF, D), 1.0, 6.0, ((0, 16), (1, 32)))
    return dict(activations=activations, out_grads=out_grads, owners=owners, weights=weights)


epsilon = 1e-6


def model_fisher(activations, out_grads, owners):
    act_float = activations.astype(jnp.float32)
    grad_float = out_grads.astype(jnp.float32)
    total = jnp.zeros((act_float.shape[1], grad_float.shape[1]), jnp.float32)
    for index in range(NSEQ):
        select = (owners == index).astype(jnp.float32)
        masked = grad_float * select[:, None]
        per_seq = jnp.dot(act_float.T, masked, precision=lax.Precision.HIGHEST)
        total = total + per_seq * per_seq
    return (total / NSEQ).astype(jnp.bfloat16)


def reference(activations, out_grads, owners, weights):
    def step(carry, inputs):
        numerator, denominator = carry
        act_one, grad_one, owner_one, weight_one = inputs
        fisher = model_fisher(act_one, grad_one, owner_one).astype(jnp.float32)
        return (numerator + fisher * weight_one.astype(jnp.float32), denominator + fisher), None

    start = jnp.zeros((weights.shape[1], weights.shape[2]), jnp.float32)
    (numerator, denominator), unused = lax.scan(step, (start, start), (activations, out_grads, owners, weights))
    return (numerator / (denominator + epsilon)).astype(jnp.bfloat16)
```

```python
import functools

import jax
import jax.numpy as jnp
from jax import lax
from jax.experimental import pallas as pl
from jax.experimental.pallas import tpu as pltpu
from jax.sharding import PartitionSpec as P

MESH = pl.DeviceIdType.MESH
F32, BF16 = jnp.float32, jnp.bfloat16
RING = 4
TOK = 4
ROWS = 448
HALF = ROWS // 2
COLS = 256
WIDE = RING * COLS
PAIR = 2 * ROWS
ACT = PAIR + 128
TILE = 32
epsilon = 1e-6


def kernel(act_ref, grad_ref, own_ref, w_ref, out_ref,
           act_msg, act_in, act_pack, act_all,
           grad_msg, grad_in, grad_pack, grad_all,
           tmp_a, tmp_b, turned, lhs, wbuf,
           zsend, far_up, far_down, near_up, near_down,
           send_sems, recv_sems, w_sems, z_sems):
    mp, shard = lax.axis_index("mp"), lax.axis_index("shard")
    y, zh = mp // RING, lax.rem(mp, RING)
    x, zl, c = shard // (2 * RING), lax.rem(shard // 2, RING), lax.rem(shard, 2)

    def at(dy=0, dzh=0, dx=0, dzl=0, dc=0):
        yy, zz = lax.rem(y + dy, RING), lax.rem(zh + dzh, RING)
        xx, ll = lax.rem(x + dx, RING), lax.rem(zl + dzl, RING)
        cc = lax.rem(c + dc, 2)
        return (yy * RING + zz, (xx * RING + ll) * 2 + cc)

    hops = [(i, j) for i in range(RING) for j in range(RING)]
    partners = [at(dy=i, dzl=j) for i, j in hops if (i, j) != (0, 0)]
    partners += [at(dy=i, dx=j) for i, j in hops if j != 0]
    partners += [at(dc=1), at(dzh=1), at(dzh=3)]

    sends = []

    def push(src, dst, recv_sem, target):
        copy = pltpu.make_async_remote_copy(
            src_ref=src, dst_ref=dst, send_sem=send_sems.at[len(sends)],
            recv_sem=recv_sem, device_id=target, device_id_type=MESH)
        copy.start()
        sends.append(copy)

    def await_all(buf, sem):
        pltpu.make_async_copy(buf, buf, sem).wait()

    barrier = pltpu.get_barrier_semaphore()
    for target in partners:
        pl.semaphore_signal(barrier, inc=1, device_id=target, device_id_type=MESH)

    rows4 = lax.broadcasted_iota(jnp.int32, (TOK, 128), 0)
    owner = jnp.zeros((TOK, 128), F32)
    for t in range(TOK):
        owner = owner + jnp.where(rows4 == t, own_ref[0, t].astype(F32), 0.0)
    for l in range(RING):
        for i in range(RING):
            col = (i * RING + l) * PAIR
            tmp_a[l, TOK * i:TOK * (i + 1), :PAIR] = act_ref[0, :, col:col + PAIR].astype(F32)
            tmp_a[l, TOK * i:TOK * (i + 1), PAIR:] = owner
        act_msg[l] = tmp_a[l].astype(BF16)
    for i in range(RING):
        for q in range(RING):
            col = i * WIDE + q * COLS
            tmp_b[i, TOK * q:TOK * (q + 1), :COLS] = grad_ref[0, :, col:col + COLS].astype(F32)
        grad_msg[i] = tmp_b[i, :, :COLS].astype(BF16)

    pl.semaphore_wait(barrier, len(partners))

    for j in range(RING):
        to = lax.rem(zl + j, RING)
        if j == 0:
            pltpu.make_async_copy(act_msg.at[to], act_in.at[zl], recv_sems.at[0]).start()
        else:
            push(act_msg.at[to], act_in.at[zl], recv_sems.at[0], at(dzl=j))
    for i, j in hops:
        to = lax.rem(y + i, RING)
        if (i, j) == (0, 0):
            pltpu.make_async_copy(grad_msg.at[to], grad_in.at[y, zl], recv_sems.at[1]).start()
        else:
            push(grad_msg.at[to], grad_in.at[y, zl], recv_sems.at[1], at(dy=i, dzl=j))

    def send_weights(d):
        slot = d % RING
        block = lax.rem(zh + slot, RING)
        for i in range(RING):
            to = lax.rem(y + i, RING)
            cols = pl.ds(pl.multiple_of(to * WIDE + block * COLS, COLS), COLS)
            src, dst = w_ref.at[0, :, cols], wbuf.at[slot, y]
            if i == 0:
                pltpu.make_async_copy(src, dst, w_sems.at[slot]).start()
            else:
                push(src, dst, w_sems.at[slot], at(dy=i))

    send_weights(2)

    await_all(act_in, recv_sems.at[0])
    for l in range(RING):
        tmp_a[l] = act_in[l].astype(F32)
    for i in range(RING):
        for l in range(RING):
            tmp_b[i, TOK * l:TOK * (l + 1), :] = tmp_a[l, TOK * i:TOK * (i + 1), :]
        act_pack[i] = tmp_b[i].astype(BF16)
    for i, j in hops:
        to = lax.rem(x + j, RING)
        if (i, j) == (0, 0):
            pltpu.make_async_copy(act_pack.at[to], act_all.at[c, y, x], recv_sems.at[2]).start()
        else:
            push(act_pack.at[to], act_all.at[c, y, x], recv_sems.at[2], at(dy=i, dx=j))

    await_all(grad_in, recv_sems.at[1])
    for i in range(RING):
        for l in range(RING):
            tmp_a[l, :, :COLS] = grad_in[i, l].astype(F32)
        for l in range(RING):
            for q in range(RING):
                tmp_b[i, TOK * l:TOK * (l + 1), COLS * q:COLS * (q + 1)] = tmp_a[l, TOK * q:TOK * (q + 1), :COLS]
        grad_pack[i] = tmp_b[i].astype(BF16)
    for j in range(RING):
        if j == 0:
            pltpu.make_async_copy(grad_pack, grad_all.at[c, x], recv_sems.at[3]).start()
        else:
            push(grad_pack, grad_all.at[c, x], recv_sems.at[3], at(dx=j))

    send_weights(1)

    await_all(act_all.at[c], recv_sems.at[2])
    push(act_all.at[c], act_all.at[c], recv_sems.at[4], at(dc=1))
    await_all(grad_all.at[c], recv_sems.at[3])
    push(grad_all.at[c], grad_all.at[c], recv_sems.at[5], at(dc=1))

    send_weights(3)
    send_weights(0)

    other = 1 - c
    await_all(act_all.at[other], recv_sems.at[4])
    mine = pl.ds(pl.multiple_of(c * 384, 128), 512)
    for i in range(RING):
        own = act_all[:, i, :, :, PAIR:].reshape(128, 128).astype(F32).T[0:1, :]
        turned[...] = act_all[:, i, :, :, mine].reshape(128, 512).astype(F32).T
        units = turned[pl.ds(pl.multiple_of(c * 64, 64), ROWS), :]
        lhs[i, 0] = (units * (1.0 - own)).astype(BF16)
        lhs[i, 1] = (units * own).astype(BF16)
    await_all(grad_all.at[other], recv_sems.at[5])

    def partial_sums(d, start, stop, sink):
        slot = d % RING
        cols = pl.ds(pl.multiple_of(lax.rem(zh + slot, RING) * COLS, COLS), COLS)

        @pl.loop(start // TILE, stop // TILE)
        def _(step):
            rows = pl.ds(pl.multiple_of(step * TILE, TILE), TILE)
            num = jnp.zeros((TILE, COLS), F32)
            den = jnp.zeros((TILE, COLS), F32)
            for i in range(RING):
                grads = grad_all[:, :, i, :, cols].reshape(128, COLS)
                one = jnp.dot(lhs[i, 0, rows, :], grads, preferred_element_type=F32)
                two = jnp.dot(lhs[i, 1, rows, :], grads, preferred_element_type=F32)
                fisher = ((one * one + two * two) * 0.5).astype(BF16).astype(F32)
                num = num + fisher * wbuf[slot, i, rows, :].astype(F32)
                den = den + fisher
            sink(rows, num, den)

    def store(at_slot):
        def sink(rows, num, den):
            zsend[at_slot, 0, rows, :] = num.astype(BF16)
            zsend[at_slot, 1, rows, :] = den.astype(BF16)
        return sink

    def store_added(at_slot, got, offset):
        def sink(rows, num, den):
            there = pl.ds(pl.multiple_of(rows.start - offset, TILE), TILE)
            zsend[at_slot, 0, rows, :] = (num + got[0, there, :].astype(F32)).astype(BF16)
            zsend[at_slot, 1, rows, :] = (den + got[1, there, :].astype(F32)).astype(BF16)
        return sink

    top, bottom = pl.ds(0, HALF), pl.ds(HALF, HALF)
    await_all(wbuf.at[2], w_sems.at[2])
    partial_sums(2, 0, HALF, store(0))
    push(zsend.at[0, :, top], far_up, z_sems.at[0], at(dzh=1))
    partial_sums(2, HALF, ROWS, store(0))
    push(zsend.at[0, :, bottom], far_down, z_sems.at[1], at(dzh=3))
    await_all(wbuf.at[1], w_sems.at[1])
    partial_sums(1, HALF, ROWS, store(1))
    push(zsend.at[1, :, bottom], near_up.at[:, bottom], z_sems.at[2], at(dzh=1))
    await_all(wbuf.at[3], w_sems.at[3])
    partial_sums(3, 0, HALF, store(2))
    push(zsend.at[2, :, top], near_down.at[:, top], z_sems.at[3], at(dzh=3))

    await_all(far_up, z_sems.at[0])
    partial_sums(1, 0, HALF, store_added(1, far_up, 0))
    push(zsend.at[1, :, top], near_up.at[:, top], z_sems.at[4], at(dzh=1))
    await_all(far_down, z_sems.at[1])
    partial_sums(3, HALF, ROWS, store_added(2, far_down, HALF))
    push(zsend.at[2, :, bottom], near_down.at[:, bottom], z_sems.at[5], at(dzh=3))

    for copy in sends[:-6]:
        copy.wait_send()
    await_all(wbuf.at[0], w_sems.at[0])
    await_all(near_up.at[:, bottom], z_sems.at[2])
    await_all(near_down.at[:, top], z_sems.at[3])
    await_all(near_up.at[:, top], z_sems.at[4])
    await_all(near_down.at[:, bottom], z_sems.at[5])

    def finish(rows, num, den):
        num = num + (near_up[0, rows, :].astype(F32) + near_down[0, rows, :].astype(F32))
        den = den + (near_up[1, rows, :].astype(F32) + near_down[1, rows, :].astype(F32))
        out_ref[rows, :] = (num / (den + epsilon)).astype(BF16)

    partial_sums(0, 0, ROWS, finish)
    for copy in sends[-6:]:
        copy.wait_send()


def per_device(activations, out_grads, owners, weights):
    vmem = pl.BlockSpec(memory_space=pltpu.VMEM)
    return pl.pallas_call(
        kernel,
        out_shape=jax.ShapeDtypeStruct((ROWS, COLS), BF16),
        in_specs=[vmem, vmem, pl.BlockSpec(memory_space=pltpu.SMEM), pl.BlockSpec(memory_space=pl.ANY)],
        out_specs=vmem,
        scratch_shapes=[
            pltpu.VMEM((RING, 16, ACT), BF16),
            pltpu.VMEM((RING, 16, ACT), BF16),
            pltpu.VMEM((RING, 16, ACT), BF16),
            pltpu.VMEM((2, RING, RING, 16, ACT), BF16),
            pltpu.VMEM((RING, 16, COLS), BF16),
            pltpu.VMEM((RING, RING, 16, COLS), BF16),
            pltpu.VMEM((RING, 16, WIDE), BF16),
            pltpu.VMEM((2, RING, RING, 16, WIDE), BF16),
            pltpu.VMEM((RING, 16, ACT), F32),
            pltpu.VMEM((RING, 16, WIDE), F32),
            pltpu.VMEM((512, 128), F32),
            pltpu.VMEM((RING, 2, ROWS, 128), BF16),
            pltpu.VMEM((RING, RING, ROWS, COLS), BF16),
            pltpu.VMEM((3, 2, ROWS, COLS), BF16),
            pltpu.VMEM((2, HALF, COLS), BF16),
            pltpu.VMEM((2, HALF, COLS), BF16),
            pltpu.VMEM((2, ROWS, COLS), BF16),
            pltpu.VMEM((2, ROWS, COLS), BF16),
            pltpu.SemaphoreType.DMA((64,)),
            pltpu.SemaphoreType.DMA((6,)),
            pltpu.SemaphoreType.DMA((RING,)),
            pltpu.SemaphoreType.DMA((6,)),
        ],
        compiler_params=pltpu.CompilerParams(
            collective_id=0, has_side_effects=True, vmem_limit_bytes=56 << 20),
    )(activations, out_grads, owners, weights)


def solution(mesh):
    return jax.shard_map(
        per_device,
        mesh=mesh,
        in_specs=(
            P("mp", "shard", None),
            P("mp", "shard", None),
            P("mp", "shard"),
            P("mp", "shard", None),
        ),
        out_specs=P("shard", "mp"),
        check_vma=False,
    )
```

```python
import jax
import jax.numpy as jnp
from jax import lax
from jax.experimental import pallas as pl
from jax.experimental.pallas import tpu as pltpu
from jax.sharding import PartitionSpec as P

MESH = pl.DeviceIdType.MESH
F32, BF16 = jnp.float32, jnp.bfloat16
RING = 4
TOK = 4
TOKENS = 128
ROWS = 448
HALF = ROWS // 2
COLS = 256
WIDE = RING * COLS
PAIR = 2 * ROWS
SIDE = 512
UNITS = ROWS + 16
CUT = 240
TILE = 32
epsilon = 1e-6


def kernel(act_ref, grad_ref, own_ref, w_ref, out_ref,
           act_msg, act_in, act_pack, act_all,
           grad_msg, grad_in, grad_pack, grad_all,
           tmp_a, tmp_b, turned, by_y, by_z, lhs, wbuf,
           zsend, far_up, far_down, near_up, near_down,
           num_own, den_own, den_send, den_in,
           send_sems, recv_sems, w_sems, z_sems):
    mp, shard = lax.axis_index("mp"), lax.axis_index("shard")
    y, zh = mp // RING, lax.rem(mp, RING)
    x, zl, c = shard // (2 * RING), lax.rem(shard // 2, RING), lax.rem(shard, 2)

    def at(dy=0, dzh=0, dx=0, dzl=0, dc=0):
        yy, zz = lax.rem(y + dy, RING), lax.rem(zh + dzh, RING)
        xx, ll = lax.rem(x + dx, RING), lax.rem(zl + dzl, RING)
        cc = lax.rem(c + dc, 2)
        return (yy * RING + zz, (xx * RING + ll) * 2 + cc)

    hops = [(i, j) for i in range(RING) for j in range(RING)]
    partners = [at(dy=i, dzl=j) for i, j in hops if (i, j) != (0, 0)]
    partners += [at(dzh=i, dzl=j) for i, j in hops if i != 0]
    partners += [at(dx=i, dc=j) for i in range(RING) for j in range(2) if (i, j) != (0, 0)]

    sends = []

    def push(src, dst, recv_sem, target):
        copy = pltpu.make_async_remote_copy(
            src_ref=src, dst_ref=dst, send_sem=send_sems.at[len(sends)],
            recv_sem=recv_sem, device_id=target, device_id_type=MESH)
        copy.start()
        sends.append(copy)

    def keep(src, dst, sem):
        pltpu.make_async_copy(src, dst, sem).start()

    def await_all(buf, sem):
        pltpu.make_async_copy(buf, buf, sem).wait()

    barrier = pltpu.get_barrier_semaphore()
    for target in partners:
        pl.semaphore_signal(barrier, inc=1, device_id=target, device_id_type=MESH)

    rows4 = lax.broadcasted_iota(jnp.int32, (TOK, 128), 0)
    low = lax.broadcasted_iota(jnp.int32, (TOK, 128), 1) < 64
    owner = jnp.zeros((TOK, 128), F32)
    for t in range(TOK):
        owner = owner + jnp.where(rows4 == t, own_ref[0, t].astype(F32), 0.0)
    for l in range(RING):
        for i in range(RING):
            col = (i * RING + l) * PAIR
            to = slice(TOK * i, TOK * (i + 1))
            middle = act_ref[0, :, col + 384:col + 512].astype(F32)
            tmp_a[l, to, 0:384] = act_ref[0, :, col:col + 384].astype(F32)
            tmp_a[l, to, 384:512] = jnp.where(low, middle, owner)
            tmp_a[l, to, 512:640] = jnp.where(low, owner, middle)
            tmp_a[l, to, 640:1024] = act_ref[0, :, col + 512:col + PAIR].astype(F32)
        act_msg[l] = tmp_a[l].astype(BF16)
    for g in range(2):
        for i in range(RING):
            for q in range(RING):
                col = i * WIDE + q * COLS if g == 0 else q * WIDE + i * COLS
                tmp_b[i, TOK * q:TOK * (q + 1), :COLS] = grad_ref[0, :, col:col + COLS].astype(F32)
            grad_msg[g, i] = tmp_b[i, :, :COLS].astype(BF16)

    pl.semaphore_wait(barrier, len(partners))

    def send_grads(g):
        ring = y if g == 0 else zh
        for i, j in hops:
            src, dst = grad_msg.at[g, lax.rem(ring + i, RING)], grad_in.at[g, ring, zl]
            if (i, j) == (0, 0):
                keep(src, dst, recv_sems.at[1 + g])
            else:
                push(src, dst, recv_sems.at[1 + g], at(dy=i, dzl=j) if g == 0 else at(dzh=i, dzl=j))

    def send_weights(d, part):
        slot, rows = d % RING, pl.ds(part * HALF, HALF)
        block = lax.rem(zh + slot, RING)
        for i in (2, 1, 3, 0):
            to = lax.rem(y + i, RING)
            cols = pl.ds(pl.multiple_of(to * WIDE + block * COLS, COLS), COLS)
            src, dst = w_ref.at[0, rows, cols], wbuf.at[slot, part, y]
            if i == 0:
                keep(src, dst, w_sems.at[2 * slot + part])
            else:
                push(src, dst, w_sems.at[2 * slot + part], at(dy=i))

    def await_weights(d, part):
        await_all(wbuf.at[d % RING, part], w_sems.at[2 * (d % RING) + part])

    for j in range(RING):
        src, dst = act_msg.at[lax.rem(zl + j, RING)], act_in.at[zl]
        if j == 0:
            keep(src, dst, recv_sems.at[0])
        else:
            push(src, dst, recv_sems.at[0], at(dzl=j))
    send_grads(0)
    send_weights(2, 0)
    send_weights(2, 1)

    await_all(act_in, recv_sems.at[0])
    for l in range(RING):
        tmp_a[l] = act_in[l].astype(F32)
    for i in range(RING):
        for l in range(RING):
            tmp_b[i, TOK * l:TOK * (l + 1), :] = tmp_a[l, TOK * i:TOK * (i + 1), :]
        for j in range(2):
            act_pack[j, i] = tmp_b[i, :, j * SIDE:(j + 1) * SIDE].astype(BF16)
    for i in range(RING):
        for j in range(2):
            src, dst = act_pack.at[lax.rem(c + j, 2), lax.rem(x + i, RING)], act_all.at[c, x]
            if (i, j) == (0, 0):
                keep(src, dst, recv_sems.at[3])
            else:
                push(src, dst, recv_sems.at[3], at(dx=i, dc=j))
    send_grads(1)

    def spread_grads(g):
        await_all(grad_in.at[g], recv_sems.at[1 + g])
        for i in range(RING):
            for l in range(RING):
                tmp_a[l, :, :COLS] = grad_in[g, i, l].astype(F32)
            for l in range(RING):
                for q in range(RING):
                    tmp_b[i, TOK * l:TOK * (l + 1), COLS * q:COLS * (q + 1)] = tmp_a[l, TOK * q:TOK * (q + 1), :COLS]
            grad_pack[g, i] = tmp_b[i].astype(BF16)
        for j in range(RING):
            if j == 0:
                keep(grad_pack.at[g], grad_all.at[g, c, x], recv_sems.at[4 + g])
            else:
                push(grad_pack.at[g], grad_all.at[g, c, x], recv_sems.at[4 + g], at(dx=j))

    spread_grads(0)

    await_all(act_all, recv_sems.at[3])
    turned[...] = act_all[...].reshape(TOKENS, SIDE).astype(F32).T
    by_z[0, :ROWS] = turned[pl.ds(pl.multiple_of(c * 64, 64), ROWS), :].astype(BF16)
    by_z[0, ROWS:] = turned[pl.ds(pl.multiple_of((1 - c) * ROWS, 64), 16), :].astype(BF16)
    keep(by_z.at[0], by_y.at[y], recv_sems.at[8])
    for i in (2, 1, 3):
        push(by_z.at[0], by_y.at[y], recv_sems.at[8], at(dy=i))
    push(by_z.at[0], by_z.at[3], recv_sems.at[9], at(dzh=1))
    push(by_z.at[0], by_z.at[1], recv_sems.at[10], at(dzh=3))
    send_weights(1, 1)
    send_weights(3, 0)
    spread_grads(1)

    def share_grads(g):
        await_all(grad_all.at[g, c], recv_sems.at[4 + g])
        push(grad_all.at[g, c], grad_all.at[g, c], recv_sems.at[6 + g], at(dc=1))

    def masked(g, i, units):
        one = units[ROWS:]
        body = units[:ROWS].reshape(ROWS // 16, 16, TOKENS)
        lhs[g, i, 0] = (body * (1 - one)[None]).reshape(ROWS, TOKENS)
        lhs[g, i, 1] = (body * one[None]).reshape(ROWS, TOKENS)

    share_grads(0)
    await_all(by_y, recv_sems.at[8])
    for i in range(RING):
        masked(0, i, by_y[i])
    await_all(grad_all.at[0, 1 - c], recv_sems.at[6])

    def fishers(g, block, rows):
        cols = pl.ds(pl.multiple_of(block * COLS, COLS), COLS)
        for i in range(RING):
            model = i if g == 0 else lax.rem(zh + i, RING)
            grads = grad_all[g, :, :, model, :, cols].reshape(TOKENS, COLS)
            one = jnp.dot(lhs[g, i, 0, rows, :], grads, preferred_element_type=F32)
            two = jnp.dot(lhs[g, i, 1, rows, :], grads, preferred_element_type=F32)
            yield ((one * one + two * two) * 0.5).astype(BF16).astype(F32)

    def numerators(d, part, sink):
        slot = d % RING

        @pl.loop(0, HALF // TILE, unroll=HALF // TILE)
        def _(step):
            there = pl.ds(pl.multiple_of(step * TILE, TILE), TILE)
            rows = pl.ds(pl.multiple_of(part * HALF + step * TILE, TILE), TILE)
            num = jnp.zeros((TILE, COLS), F32)
            for i, fisher in enumerate(fishers(0, lax.rem(zh + slot, RING), rows)):
                num = num + fisher * wbuf[slot, part, i, there, :].astype(F32)
            sink(rows, there, num)

    def store(slot, got=None):
        def sink(rows, there, num):
            if got is not None:
                num = num + got[there, :].astype(F32)
            zsend[slot, rows, :] = num.astype(BF16)
        return sink

    top, bottom = pl.ds(0, HALF), pl.ds(HALF, HALF)
    await_weights(2, 0)
    numerators(2, 0, store(0))
    push(zsend.at[0, top], far_up, z_sems.at[0], at(dzh=1))
    await_weights(2, 1)
    numerators(2, 1, store(0))
    push(zsend.at[0, bottom], far_down, z_sems.at[1], at(dzh=3))
    send_weights(1, 0)
    send_weights(3, 1)
    share_grads(1)
    await_weights(1, 1)
    numerators(1, 1, store(1))
    push(zsend.at[1, bottom], near_up.at[bottom], z_sems.at[2], at(dzh=1))
    await_weights(3, 0)
    numerators(3, 0, store(2))
    push(zsend.at[2, top], near_down.at[top], z_sems.at[3], at(dzh=3))
    send_weights(0, 0)
    send_weights(0, 1)

    await_all(by_z.at[3], recv_sems.at[9])
    push(by_z.at[3, :CUT], by_z.at[2, :CUT], recv_sems.at[11], at(dzh=1))
    await_all(by_z.at[1], recv_sems.at[10])
    push(by_z.at[1, CUT:], by_z.at[2, CUT:], recv_sems.at[12], at(dzh=3))

    await_all(far_up, z_sems.at[0])
    await_weights(1, 0)
    numerators(1, 0, store(1, far_up))
    push(zsend.at[1, top], near_up.at[top], z_sems.at[4], at(dzh=1))
    await_all(far_down, z_sems.at[1])
    await_weights(3, 1)
    numerators(3, 1, store(2, far_down))
    push(zsend.at[2, bottom], near_down.at[bottom], z_sems.at[5], at(dzh=3))

    await_all(grad_all.at[1, 1 - c], recv_sems.at[7])
    for i in (0, 1, 3):
        masked(1, i, by_z[i])
    await_all(by_z.at[2, :CUT], recv_sems.at[11])
    await_all(by_z.at[2, CUT:], recv_sems.at[12])
    masked(1, 2, by_z[2])
    for i in (2, 1, 3, 0):
        @pl.loop(0, ROWS // TILE, unroll=HALF // TILE)
        def _(step, i=i):
            rows = pl.ds(pl.multiple_of(step * TILE, TILE), TILE)
            den = jnp.zeros((TILE, COLS), F32)
            for fisher in fishers(1, lax.rem(y + i, RING), rows):
                den = den + fisher
            if i == 0:
                den_own[rows, :] = den
            else:
                den_send[i - 1, rows, :] = den.astype(BF16)
        if i != 0:
            push(den_send.at[i - 1], den_in.at[i - 1], recv_sems.at[13], at(dy=i))

    for part in range(2):
        def hold(rows, there, num):
            num_own[rows, :] = num
        await_weights(0, part)
        numerators(0, part, hold)

    for copy in sends[:-5]:
        copy.wait_send()
    await_all(den_in, recv_sems.at[13])
    await_all(near_up.at[bottom], z_sems.at[2])
    await_all(near_down.at[top], z_sems.at[3])
    await_all(near_up.at[top], z_sems.at[4])
    await_all(near_down.at[bottom], z_sems.at[5])

    @pl.loop(0, ROWS // TILE, unroll=HALF // TILE)
    def _(step):
        rows = pl.ds(pl.multiple_of(step * TILE, TILE), TILE)
        num = num_own[rows, :] + (near_up[rows, :].astype(F32) + near_down[rows, :].astype(F32))
        den = den_own[rows, :]
        for i in range(RING - 1):
            den = den + den_in[i, rows, :].astype(F32)
        out_ref[rows, :] = (num / (den + epsilon)).astype(BF16)

    for copy in sends[-5:]:
        copy.wait_send()


def per_device(activations, out_grads, owners, weights):
    vmem = pl.BlockSpec(memory_space=pltpu.VMEM)
    return pl.pallas_call(
        kernel,
        out_shape=jax.ShapeDtypeStruct((ROWS, COLS), BF16),
        in_specs=[vmem, vmem, pl.BlockSpec(memory_space=pltpu.SMEM), pl.BlockSpec(memory_space=pl.ANY)],
        out_specs=vmem,
        scratch_shapes=[
            pltpu.VMEM((RING, 16, 2 * SIDE), BF16),
            pltpu.VMEM((RING, 16, 2 * SIDE), BF16),
            pltpu.VMEM((2, RING, 16, SIDE), BF16),
            pltpu.VMEM((2, RING, 16, SIDE), BF16),
            pltpu.VMEM((2, RING, 16, COLS), BF16),
            pltpu.VMEM((2, RING, RING, 16, COLS), BF16),
            pltpu.VMEM((2, RING, 16, WIDE), BF16),
            pltpu.VMEM((2, 2, RING, RING, 16, WIDE), BF16),
            pltpu.VMEM((RING, 16, WIDE), F32),
            pltpu.VMEM((RING, 16, WIDE), F32),
            pltpu.VMEM((SIDE, TOKENS), F32),
            pltpu.VMEM((RING, UNITS, TOKENS), BF16),
            pltpu.VMEM((RING, UNITS, TOKENS), BF16),
            pltpu.VMEM((2, RING, 2, ROWS, TOKENS), BF16),
            pltpu.VMEM((RING, 2, RING, HALF, COLS), BF16),
            pltpu.VMEM((3, ROWS, COLS), BF16),
            pltpu.VMEM((HALF, COLS), BF16),
            pltpu.VMEM((HALF, COLS), BF16),
            pltpu.VMEM((ROWS, COLS), BF16),
            pltpu.VMEM((ROWS, COLS), BF16),
            pltpu.VMEM((ROWS, COLS), F32),
            pltpu.VMEM((ROWS, COLS), F32),
            pltpu.VMEM((3, ROWS, COLS), BF16),
            pltpu.VMEM((3, ROWS, COLS), BF16),
            pltpu.SemaphoreType.DMA((96,)),
            pltpu.SemaphoreType.DMA((14,)),
            pltpu.SemaphoreType.DMA((2 * RING,)),
            pltpu.SemaphoreType.DMA((6,)),
        ],
        compiler_params=pltpu.CompilerParams(
            collective_id=0, has_side_effects=True, vmem_limit_bytes=56 << 20),
    )(activations, out_grads, owners, weights)


def solution(mesh):
    return jax.shard_map(
        per_device,
        mesh=mesh,
        in_specs=(
            P("mp", "shard", None),
            P("mp", "shard", None),
            P("mp", "shard"),
            P("mp", "shard", None),
        ),
        out_specs=P("shard", "mp"),
        check_vma=False,
    )
```

```python
import jax
import jax.numpy as jnp
from jax import lax
from jax.experimental import pallas as pl
from jax.experimental.pallas import tpu as pltpu
from jax.sharding import PartitionSpec as P

MESH = pl.DeviceIdType.MESH
F32, BF16 = jnp.float32, jnp.bfloat16
RING = 4
TOK = 4
TOKENS = 128
ROWS = 448
HALF = ROWS // 2
COLS = 256
WIDE = RING * COLS
PAIR = 2 * ROWS
SIDE = 512
UNITS = ROWS + 16
CUT = 240
TILE = 32
epsilon = 1e-6


def kernel(act_hbm, grad_hbm, own_ref, w_ref, out_ref,
           act_ref, grad_ref,
           act_msg, act_in, act_pack, act_all,
           grad_msg, grad_in, grad_pack, grad_all,
           tmp_a, tmp_b, turned, by_y, by_z, lhs, wbuf, wown,
           ring_send, far_in, near_in, num_own, den_own,
           send_sems, recv_sems, w_sems, own_sems, ring_sems, grad_sems):
    mp, shard = lax.axis_index("mp"), lax.axis_index("shard")
    y, zh = mp // RING, lax.rem(mp, RING)
    x, zl, c = shard // (2 * RING), lax.rem(shard // 2, RING), lax.rem(shard, 2)

    def at(dy=0, dzh=0, dx=0, dzl=0, dc=0):
        yy, zz = lax.rem(y + dy, RING), lax.rem(zh + dzh, RING)
        xx, ll = lax.rem(x + dx, RING), lax.rem(zl + dzl, RING)
        cc = lax.rem(c + dc, 2)
        return (yy * RING + zz, (xx * RING + ll) * 2 + cc)

    hops = [(i, j) for i in range(RING) for j in range(RING)]
    partners = [at(dy=i, dzl=j) for i, j in hops if (i, j) != (0, 0)]
    partners += [at(dzh=i, dzl=j) for i, j in hops if i != 0]
    partners += [at(dx=i, dc=j) for i in range(RING) for j in range(2) if (i, j) != (0, 0)]

    sends = []

    def push(src, dst, recv_sem, target):
        copy = pltpu.make_async_remote_copy(
            src_ref=src, dst_ref=dst, send_sem=send_sems.at[len(sends)],
            recv_sem=recv_sem, device_id=target, device_id_type=MESH)
        copy.start()
        sends.append(copy)

    def keep(src, dst, sem):
        pltpu.make_async_copy(src, dst, sem).start()

    def await_all(buf, sem):
        pltpu.make_async_copy(buf, buf, sem).wait()

    inputs = (pltpu.make_async_copy(act_hbm, act_ref, recv_sems.at[4]),
              pltpu.make_async_copy(grad_hbm, grad_ref, recv_sems.at[5]))
    for copy in inputs:
        copy.start()
    barrier = pltpu.get_barrier_semaphore()
    for target in partners:
        pl.semaphore_signal(barrier, inc=1, device_id=target, device_id_type=MESH)

    rows4 = lax.broadcasted_iota(jnp.int32, (TOK, 128), 0)
    low = lax.broadcasted_iota(jnp.int32, (TOK, 128), 1) < 64
    owner = jnp.zeros((TOK, 128), F32)
    for t in range(TOK):
        owner = owner + jnp.where(rows4 == t, own_ref[0, t].astype(F32), 0.0)
    for copy in inputs:
        copy.wait()
    for l in range(RING):
        for i in range(RING):
            col = (i * RING + l) * PAIR
            to = slice(TOK * i, TOK * (i + 1))
            middle = act_ref[0, :, col + 384:col + 512].astype(F32)
            tmp_a[l, to, 0:384] = act_ref[0, :, col:col + 384].astype(F32)
            tmp_a[l, to, 384:512] = jnp.where(low, middle, owner)
            tmp_a[l, to, 512:640] = jnp.where(low, owner, middle)
            tmp_a[l, to, 640:1024] = act_ref[0, :, col + 512:col + PAIR].astype(F32)
        act_msg[l] = tmp_a[l].astype(BF16)
    for g in range(2):
        for i in range(RING):
            for q in range(RING):
                col = i * WIDE + q * COLS if g == 0 else q * WIDE + i * COLS
                tmp_b[i, TOK * q:TOK * (q + 1), :COLS] = grad_ref[0, :, col:col + COLS].astype(F32)
            grad_msg[g, i] = tmp_b[i, :, :COLS].astype(BF16)

    pl.semaphore_wait(barrier, len(partners))

    def send_grads(g):
        ring = y if g == 0 else zh
        for i, j in hops:
            src, dst = grad_msg.at[g, lax.rem(ring + i, RING)], grad_in.at[g, ring, zl]
            if (i, j) == (0, 0):
                keep(src, dst, recv_sems.at[1 + g])
            else:
                push(src, dst, recv_sems.at[1 + g], at(dy=i, dzl=j) if g == 0 else at(dzh=i, dzl=j))

    def send_weights(d, part):
        slot, rows = d % RING, pl.ds(part * HALF, HALF)
        block = lax.rem(zh + slot, RING)
        for i in (2, 1, 3, 0):
            to = lax.rem(y + i, RING)
            cols = pl.ds(pl.multiple_of(to * WIDE + block * COLS, COLS), COLS)
            src, dst = w_ref.at[0, rows, cols], wbuf.at[slot - 1, part, y]
            if i == 0:
                keep(src, dst, w_sems.at[2 * slot + part])
            else:
                push(src, dst, w_sems.at[2 * slot + part], at(dy=i))

    def await_weights(d, part):
        await_all(wbuf.at[d - 1, part], w_sems.at[2 * d + part])

    for j in range(RING):
        src, dst = act_msg.at[lax.rem(zl + j, RING)], act_in.at[zl]
        if j == 0:
            keep(src, dst, recv_sems.at[0])
        else:
            push(src, dst, recv_sems.at[0], at(dzl=j))
    send_weights(2, 0)
    send_weights(2, 1)

    await_all(act_in, recv_sems.at[0])
    for l in range(RING):
        tmp_a[l] = act_in[l].astype(F32)
    for i in range(RING):
        for l in range(RING):
            tmp_b[i, TOK * l:TOK * (l + 1), :] = tmp_a[l, TOK * i:TOK * (i + 1), :]
        for j in range(2):
            act_pack[j, i] = tmp_b[i, :, j * SIDE:(j + 1) * SIDE].astype(BF16)
    for i in range(RING):
        for j in range(2):
            src, dst = act_pack.at[lax.rem(c + j, 2), lax.rem(x + i, RING)], act_all.at[c, x]
            if (i, j) == (0, 0):
                keep(src, dst, recv_sems.at[3])
            else:
                push(src, dst, recv_sems.at[3], at(dx=i, dc=j))
    send_grads(0)

    def pack_grads(g):
        await_all(grad_in.at[g], recv_sems.at[1 + g])
        for i in range(RING):
            for l in range(RING):
                tmp_a[l, :, :COLS] = grad_in[g, i, l].astype(F32)
            for l in range(RING):
                for q in range(RING):
                    tmp_b[i, TOK * l:TOK * (l + 1), COLS * q:COLS * (q + 1)] = tmp_a[l, TOK * q:TOK * (q + 1), :COLS]
            grad_pack[g, i] = tmp_b[i].astype(BF16)

    def grad_block(g, k):
        return pl.ds(pl.multiple_of(lax.rem((y if g else zh) + k, RING) * COLS, COLS), COLS)

    def spread_grads(g, k):
        src = grad_pack.at[g, :, :, grad_block(g, k)]
        dst = grad_all.at[g, c, x, :, :, grad_block(g, k)]
        keep(src, dst, grad_sems.at[g, 0, k])
        for i in (2, 1, 3):
            push(src, dst, grad_sems.at[g, 0, k], at(dx=i))

    def share_grads(g, k):
        both = grad_all.at[g, c, :, :, :, grad_block(g, k)]
        await_all(both, grad_sems.at[g, 0, k])
        push(both, both, grad_sems.at[g, 1, k], at(dc=1))

    def await_grads(g, k):
        await_all(grad_all.at[g, 1 - c, :, :, :, grad_block(g, k)], grad_sems.at[g, 1, k])

    await_all(act_all, recv_sems.at[3])
    turned[...] = act_all[...].reshape(TOKENS, SIDE).astype(F32).T
    by_z[0, :ROWS] = turned[pl.ds(pl.multiple_of(c * 64, 64), ROWS), :].astype(BF16)
    by_z[0, ROWS:] = turned[pl.ds(pl.multiple_of((1 - c) * ROWS, 64), 16), :].astype(BF16)
    keep(by_z.at[0], by_y.at[y], recv_sems.at[8])
    for i in (2, 1, 3):
        push(by_z.at[0], by_y.at[y], recv_sems.at[8], at(dy=i))
    push(by_z.at[0], by_z.at[3], recv_sems.at[9], at(dzh=1))
    push(by_z.at[0], by_z.at[1], recv_sems.at[10], at(dzh=3))
    pack_grads(0)
    for k in (2, 1, 3):
        spread_grads(0, k)
    send_weights(1, 1)
    send_weights(3, 0)
    send_grads(1)
    for i in (2, 1, 3, 0):
        cols = lax.rem(y + i, RING) * WIDE + zh * COLS
        keep(w_ref.at[0, :, pl.ds(pl.multiple_of(cols, COLS), COLS)], wown.at[i], own_sems.at[i])

    def masked(g, i, units):
        one = units[ROWS:]
        body = units[:ROWS].reshape(ROWS // 16, 16, TOKENS)
        lhs[g, i, 0] = (body * (1 - one)[None]).reshape(ROWS, TOKENS)
        lhs[g, i, 1] = (body * one[None]).reshape(ROWS, TOKENS)

    share_grads(0, 2)
    await_all(by_y, recv_sems.at[8])
    for i in range(RING):
        masked(0, i, by_y[i])
    await_grads(0, 2)

    def fishers(g, block, rows, models=RING):
        cols = pl.ds(pl.multiple_of(block * COLS, COLS), COLS)
        for i in range(models):
            model = i if g == 0 else lax.rem(zh + i, RING)
            grads = grad_all[g, :, :, model, :, cols].reshape(TOKENS, COLS)
            one = jnp.dot(lhs[g, i, 0, rows, :], grads, preferred_element_type=F32)
            two = jnp.dot(lhs[g, i, 1, rows, :], grads, preferred_element_type=F32)
            yield ((one * one + two * two) * 0.5).astype(BF16).astype(F32)

    def over_rows(part, body):
        @pl.loop(0, HALF // TILE, unroll=HALF // TILE)
        def _(step):
            there = pl.ds(pl.multiple_of(step * TILE, TILE), TILE)
            rows = pl.ds(pl.multiple_of(part * HALF + step * TILE, TILE), TILE)
            body(rows, there)

    def y_ring_numerators(d, part, rows, there):
        num = jnp.zeros((TILE, COLS), F32)
        for i, fisher in enumerate(fishers(0, lax.rem(zh + d, RING), rows)):
            num = num + fisher * wbuf[d - 1, part, i, there, :].astype(F32)
        return num

    def own_numerators(d, part, rows, there):
        for fisher in fishers(1, lax.rem(y + d, RING), rows, 1):
            return fisher * wown[d, rows, :].astype(F32)

    def denominators(d, part, rows, there):
        den = jnp.zeros((TILE, COLS), F32)
        for fisher in fishers(1, lax.rem(y + d, RING), rows):
            den = den + fisher
        return den

    terms = (y_ring_numerators, own_numerators, denominators)

    def step_to(r, d):
        return at(dzh=d) if r == 0 else at(dy=d)

    def give(r, d, part, got=None):
        slot = d - 1

        def body(rows, there):
            value = terms[r](d, part, rows, there)
            if got is not None:
                value = value + got[there, :].astype(F32)
            ring_send[r, slot, rows, :] = value.astype(BF16)
        over_rows(part, body)
        src = ring_send.at[r, slot, pl.ds(part * HALF, HALF)]
        if d == 2:
            push(src, far_in.at[r, part], ring_sems.at[r, part], step_to(r, 1 if part == 0 else 3))
        else:
            side = 0 if d == 1 else 1
            push(src, near_in.at[r, side, part], ring_sems.at[r, 2 + 2 * side + part], step_to(r, d))

    def give_added(r, d):
        part = 0 if d == 1 else 1
        await_all(far_in.at[r, part], ring_sems.at[r, part])
        give(r, d, part, far_in.at[r, part])

    def received(r, part, there):
        return near_in[r, 0, part, there, :].astype(F32) + near_in[r, 1, part, there, :].astype(F32)

    await_weights(2, 0)
    give(0, 2, 0)
    await_weights(2, 1)
    give(0, 2, 1)
    send_weights(1, 0)
    send_weights(3, 1)
    share_grads(0, 1)
    share_grads(0, 3)
    pack_grads(1)
    for k in (2, 1, 3, 0):
        spread_grads(1, k)

    await_all(by_z.at[3], recv_sems.at[9])
    push(by_z.at[3, :CUT], by_z.at[2, :CUT], recv_sems.at[11], at(dzh=1))
    await_all(by_z.at[1], recv_sems.at[10])
    push(by_z.at[1, CUT:], by_z.at[2, CUT:], recv_sems.at[12], at(dzh=3))

    for k in (2, 1, 3, 0):
        share_grads(1, k)
    await_weights(1, 1)
    await_grads(0, 1)
    give(0, 1, 1)
    await_weights(3, 0)
    await_grads(0, 3)
    give(0, 3, 0)
    for i in (0, 1, 3):
        masked(1, i, by_z[i])
    for i in (2, 1, 3, 0):
        await_all(wown.at[i], own_sems.at[i])
    await_grads(1, 2)
    give(1, 2, 0)
    give(1, 2, 1)
    await_grads(1, 1)
    give(1, 1, 1)
    await_grads(1, 3)
    give(1, 3, 0)
    await_all(by_z.at[2, :CUT], recv_sems.at[11])
    await_all(by_z.at[2, CUT:], recv_sems.at[12])
    masked(1, 2, by_z[2])
    give(2, 2, 0)
    give(2, 2, 1)
    give(2, 1, 1)
    give(2, 3, 0)
    await_weights(1, 0)
    give_added(0, 1)
    await_weights(3, 1)
    give_added(0, 3)
    give_added(1, 1)
    give_added(1, 3)
    await_grads(1, 0)
    for part in range(2):
        def hold(rows, there, part=part):
            num_own[rows, :] = own_numerators(0, part, rows, there)
            den_own[rows, :] = denominators(0, part, rows, there)
        over_rows(part, hold)
    give_added(2, 1)
    give_added(2, 3)

    for copy in sends[:-5]:
        copy.wait_send()
    for part in range(2):
        for r in range(3):
            for side in range(2):
                await_all(near_in.at[r, side, part], ring_sems.at[r, 2 + 2 * side + part])

        def finish(rows, there, part=part):
            num = num_own[rows, :] + (received(0, part, there) + received(1, part, there))
            den = den_own[rows, :] + received(2, part, there)
            out_ref[rows, :] = (num / (den + epsilon)).astype(BF16)
        over_rows(part, finish)

    for copy in sends[-5:]:
        copy.wait_send()


def per_device(activations, out_grads, owners, weights):
    hbm, vmem = pl.BlockSpec(memory_space=pl.ANY), pl.BlockSpec(memory_space=pltpu.VMEM)
    return pl.pallas_call(
        kernel,
        out_shape=jax.ShapeDtypeStruct((ROWS, COLS), BF16),
        in_specs=[hbm, hbm, pl.BlockSpec(memory_space=pltpu.SMEM), hbm],
        out_specs=vmem,
        scratch_shapes=[
            pltpu.VMEM(activations.shape, BF16),
            pltpu.VMEM(out_grads.shape, BF16),
            pltpu.VMEM((RING, 16, 2 * SIDE), BF16),
            pltpu.VMEM((RING, 16, 2 * SIDE), BF16),
            pltpu.VMEM((2, RING, 16, SIDE), BF16),
            pltpu.VMEM((2, RING, 16, SIDE), BF16),
            pltpu.VMEM((2, RING, 16, COLS), BF16),
            pltpu.VMEM((2, RING, RING, 16, COLS), BF16),
            pltpu.VMEM((2, RING, 16, WIDE), BF16),
            pltpu.VMEM((2, 2, RING, RING, 16, WIDE), BF16),
            pltpu.VMEM((RING, 16, WIDE), F32),
            pltpu.VMEM((RING, 16, WIDE), F32),
            pltpu.VMEM((SIDE, TOKENS), F32),
            pltpu.VMEM((RING, UNITS, TOKENS), BF16),
            pltpu.VMEM((RING, UNITS, TOKENS), BF16),
            pltpu.VMEM((2, RING, 2, ROWS, TOKENS), BF16),
            pltpu.VMEM((RING - 1, 2, RING, HALF, COLS), BF16),
            pltpu.VMEM((RING, ROWS, COLS), BF16),
            pltpu.VMEM((3, 3, ROWS, COLS), BF16),
            pltpu.VMEM((3, 2, HALF, COLS), BF16),
            pltpu.VMEM((3, 2, 2, HALF, COLS), BF16),
            pltpu.VMEM((ROWS, COLS), F32),
            pltpu.VMEM((ROWS, COLS), F32),
            pltpu.SemaphoreType.DMA((128,)),
            pltpu.SemaphoreType.DMA((14,)),
            pltpu.SemaphoreType.DMA((2 * RING,)),
            pltpu.SemaphoreType.DMA((RING,)),
            pltpu.SemaphoreType.DMA((3, 6)),
            pltpu.SemaphoreType.DMA((2, 2, RING)),
        ],
        compiler_params=pltpu.CompilerParams(
            collective_id=0, has_side_effects=True, vmem_limit_bytes=56 << 20),
    )(activations, out_grads, owners, weights)


def solution(mesh):
    return jax.shard_map(
        per_device,
        mesh=mesh,
        in_specs=(
            P("mp", "shard", None),
            P("mp", "shard", None),
            P("mp", "shard"),
            P("mp", "shard", None),
        ),
        out_specs=P("shard", "mp"),
        check_vma=False,
    )
```

```python
import jax
import jax.numpy as jnp
from jax import lax
from jax.experimental import pallas as pl
from jax.experimental.pallas import tpu as pltpu
from jax.sharding import PartitionSpec as P

MESH = pl.DeviceIdType.MESH
F32, BF16 = jnp.float32, jnp.bfloat16
RING = 4
TOK = 4
TOKENS = 128
ROWS = 448
HALF = ROWS // 2
COLS = 256
WIDE = RING * COLS
PAIR = 2 * ROWS
SIDE = 512
UNITS = ROWS + 16
CUT = 240
TILE = 112
epsilon = 1e-6


def kernel(act_hbm, grad_hbm, own_ref, w_ref, out_ref,
           act_ref, grad_ref,
           act_msg, act_in, act_pack, act_all,
           grad_msg, grad_step, grad_in, grad_pack, grad_all,
           tmp_a, tmp_b, turned, by_y, by_z, lhs, wbuf, wown,
           ring_send, far_in, near_in, num_own, den_own,
           send_sems, recv_sems, w_sems, own_sems, ring_sems, grad_sems):
    mp, shard = lax.axis_index("mp"), lax.axis_index("shard")
    y, zh = mp // RING, lax.rem(mp, RING)
    x, zl, c = shard // (2 * RING), lax.rem(shard // 2, RING), lax.rem(shard, 2)

    def at(dy=0, dzh=0, dx=0, dzl=0, dc=0):
        yy, zz = lax.rem(y + dy, RING), lax.rem(zh + dzh, RING)
        xx, ll = lax.rem(x + dx, RING), lax.rem(zl + dzl, RING)
        cc = lax.rem(c + dc, 2)
        return (yy * RING + zz, (xx * RING + ll) * 2 + cc)

    partners = [at(dy=i) for i in range(1, RING)] + [at(dzl=i) for i in range(1, RING)]
    partners += [at(dzh=i) for i in range(1, RING)]
    partners += [at(dx=i, dc=j) for i in range(RING) for j in range(2) if (i, j) != (0, 0)]

    sends = []

    def push(src, dst, recv_sem, target):
        copy = pltpu.make_async_remote_copy(
            src_ref=src, dst_ref=dst, send_sem=send_sems.at[len(sends)],
            recv_sem=recv_sem, device_id=target, device_id_type=MESH)
        copy.start()
        sends.append(copy)

    def keep(src, dst, sem):
        pltpu.make_async_copy(src, dst, sem).start()

    def await_all(buf, sem):
        pltpu.make_async_copy(buf, buf, sem).wait()

    inputs = (pltpu.make_async_copy(act_hbm, act_ref, recv_sems.at[4]),
              pltpu.make_async_copy(grad_hbm, grad_ref, recv_sems.at[5]))
    for copy in inputs:
        copy.start()
    barrier = pltpu.get_barrier_semaphore()
    for target in partners:
        pl.semaphore_signal(barrier, inc=1, device_id=target, device_id_type=MESH)

    rows4 = lax.broadcasted_iota(jnp.int32, (TOK, 128), 0)
    low = lax.broadcasted_iota(jnp.int32, (TOK, 128), 1) < 64
    owner = jnp.zeros((TOK, 128), F32)
    for t in range(TOK):
        owner = owner + jnp.where(rows4 == t, own_ref[0, t].astype(F32), 0.0)
    inputs[0].wait()
    for l in range(RING):
        for i in range(RING):
            col = (i * RING + l) * PAIR
            to = slice(TOK * i, TOK * (i + 1))
            middle = act_ref[0, :, col + 384:col + 512].astype(F32)
            tmp_a[l, to, 0:384] = act_ref[0, :, col:col + 384].astype(F32)
            tmp_a[l, to, 384:512] = jnp.where(low, middle, owner)
            tmp_a[l, to, 512:640] = jnp.where(low, owner, middle)
            tmp_a[l, to, 640:1024] = act_ref[0, :, col + 512:col + PAIR].astype(F32)
        act_msg[l] = tmp_a[l].astype(BF16)
    pl.semaphore_wait(barrier, len(partners))

    def send_grads(g):
        ring = zh if g else y
        for i in range(RING):
            src, dst = grad_msg.at[g, lax.rem(ring + i, RING)], grad_step.at[g, ring]
            if i == 0:
                keep(src, dst, recv_sems.at[6 + g])
            else:
                push(src, dst, recv_sems.at[6 + g], at(dzh=i) if g else at(dy=i))

    def send_grads_on(g):
        await_all(grad_step.at[g], recv_sems.at[6 + g])
        for j in range(RING):
            src, dst = grad_step.at[g], grad_in.at[g, :, zl]
            if j == 0:
                keep(src, dst, recv_sems.at[1 + g])
            else:
                push(src, dst, recv_sems.at[1 + g], at(dzl=j))

    def send_weights(d, part):
        slot, rows = d % RING, pl.ds(part * HALF, HALF)
        block = lax.rem(zh + slot, RING)
        for i in (2, 1, 3, 0):
            to = lax.rem(y + i, RING)
            cols = pl.ds(pl.multiple_of(to * WIDE + block * COLS, COLS), COLS)
            src, dst = w_ref.at[0, rows, cols], wbuf.at[slot - 1, part, y]
            if i == 0:
                keep(src, dst, w_sems.at[2 * slot + part])
            else:
                push(src, dst, w_sems.at[2 * slot + part], at(dy=i))

    def await_weights(d, part):
        await_all(wbuf.at[d - 1, part], w_sems.at[2 * d + part])

    for j in range(RING):
        src, dst = act_msg.at[lax.rem(zl + j, RING)], act_in.at[zl]
        if j == 0:
            keep(src, dst, recv_sems.at[0])
        else:
            push(src, dst, recv_sems.at[0], at(dzl=j))
    inputs[1].wait()
    for g in range(2):
        for i in range(RING):
            for q in range(RING):
                col = i * WIDE + q * COLS if g == 0 else q * WIDE + i * COLS
                tmp_b[i, TOK * q:TOK * (q + 1), :COLS] = grad_ref[0, :, col:col + COLS].astype(F32)
            grad_msg[g, i] = tmp_b[i, :, :COLS].astype(BF16)
    send_grads(0)
    send_grads(1)
    send_weights(2, 0)
    send_weights(2, 1)

    await_all(act_in, recv_sems.at[0])
    for l in range(RING):
        tmp_a[l] = act_in[l].astype(F32)
    for i in range(RING):
        for l in range(RING):
            tmp_b[i, TOK * l:TOK * (l + 1), :] = tmp_a[l, TOK * i:TOK * (i + 1), :]
        for j in range(2):
            act_pack[j, i] = tmp_b[i, :, j * SIDE:(j + 1) * SIDE].astype(BF16)
    for i in range(RING):
        for j in range(2):
            src, dst = act_pack.at[lax.rem(c + j, 2), lax.rem(x + i, RING)], act_all.at[c, x]
            if (i, j) == (0, 0):
                keep(src, dst, recv_sems.at[3])
            else:
                push(src, dst, recv_sems.at[3], at(dx=i, dc=j))
    send_grads_on(0)

    def pack_grads(g):
        await_all(grad_in.at[g], recv_sems.at[1 + g])
        for i in range(RING):
            for l in range(RING):
                tmp_a[l, :, :COLS] = grad_in[g, i, l].astype(F32)
            for l in range(RING):
                for q in range(RING):
                    tmp_b[i, TOK * l:TOK * (l + 1), COLS * q:COLS * (q + 1)] = tmp_a[l, TOK * q:TOK * (q + 1), :COLS]
            grad_pack[g, i] = tmp_b[i].astype(BF16)

    def grad_block(g, k):
        return pl.ds(pl.multiple_of(lax.rem((y if g else zh) + k, RING) * COLS, COLS), COLS)

    def spread_grads(g, k):
        src = grad_pack.at[g, :, :, grad_block(g, k)]
        dst = grad_all.at[g, c, x, :, :, grad_block(g, k)]
        keep(src, dst, grad_sems.at[g, 0, k])
        for i in (2, 1, 3):
            push(src, dst, grad_sems.at[g, 0, k], at(dx=i))

    def share_grads(g, k):
        both = grad_all.at[g, c, :, :, :, grad_block(g, k)]
        await_all(both, grad_sems.at[g, 0, k])
        push(both, both, grad_sems.at[g, 1, k], at(dc=1))

    def await_grads(g, k):
        await_all(grad_all.at[g, 1 - c, :, :, :, grad_block(g, k)], grad_sems.at[g, 1, k])

    await_all(act_all, recv_sems.at[3])
    turned[...] = act_all[...].reshape(TOKENS, SIDE).astype(F32).T
    by_z[0, :ROWS] = turned[pl.ds(pl.multiple_of(c * 64, 64), ROWS), :].astype(BF16)
    by_z[0, ROWS:] = turned[pl.ds(pl.multiple_of((1 - c) * ROWS, 64), 16), :].astype(BF16)
    push(by_z.at[0], by_z.at[3], recv_sems.at[9], at(dzh=1))
    push(by_z.at[0], by_z.at[1], recv_sems.at[10], at(dzh=3))
    for i in (2, 1, 3):
        push(by_z.at[0], by_y.at[y], recv_sems.at[8], at(dy=i))
    keep(by_z.at[0], by_y.at[y], recv_sems.at[8])
    pack_grads(0)
    for k in (2, 1, 3):
        spread_grads(0, k)
    send_weights(1, 1)
    send_weights(3, 0)
    send_grads_on(1)
    for i in (2, 1, 3, 0):
        cols = lax.rem(y + i, RING) * WIDE + zh * COLS
        keep(w_ref.at[0, :, pl.ds(pl.multiple_of(cols, COLS), COLS)], wown.at[i], own_sems.at[i])

    def masked(g, i, units):
        one = units[ROWS:]
        body = units[:ROWS].reshape(ROWS // 16, 16, TOKENS)
        lhs[g, i, 0] = (body * (1 - one)[None]).reshape(ROWS, TOKENS)
        lhs[g, i, 1] = (body * one[None]).reshape(ROWS, TOKENS)

    share_grads(0, 2)
    await_all(by_y, recv_sems.at[8])
    for i in range(RING):
        masked(0, i, by_y[i])
    await_grads(0, 2)

    def fishers(g, block, rows, models=RING):
        cols = pl.ds(pl.multiple_of(block * COLS, COLS), COLS)
        for i in range(models):
            model = i if g == 0 else lax.rem(zh + i, RING)
            grads = grad_all[g, :, :, model, :, cols].reshape(TOKENS, COLS)
            one = jnp.dot(lhs[g, i, 0, rows, :], grads, preferred_element_type=F32)
            two = jnp.dot(lhs[g, i, 1, rows, :], grads, preferred_element_type=F32)
            yield ((one * one + two * two) * 0.5).astype(BF16).astype(F32)

    def over_rows(part, body):
        @pl.loop(0, HALF // TILE, unroll=1)
        def _(step):
            there = pl.ds(pl.multiple_of(step * TILE, TILE), TILE)
            rows = pl.ds(pl.multiple_of(part * HALF + step * TILE, TILE), TILE)
            body(rows, there)

    def y_ring_numerators(d, part, rows, there):
        num = jnp.zeros((TILE, COLS), F32)
        for i, fisher in enumerate(fishers(0, lax.rem(zh + d, RING), rows)):
            num = num + fisher * wbuf[d - 1, part, i, there, :].astype(F32)
        return num

    def own_numerators(d, part, rows, there):
        for fisher in fishers(1, lax.rem(y + d, RING), rows, 1):
            return fisher * wown[d, rows, :].astype(F32)

    def denominators(d, part, rows, there):
        den = jnp.zeros((TILE, COLS), F32)
        for fisher in fishers(1, lax.rem(y + d, RING), rows):
            den = den + fisher
        return den

    terms = (y_ring_numerators, own_numerators, denominators)

    def step_to(r, d):
        return at(dzh=d) if r == 0 else at(dy=d)

    def give(r, d, part, got=None):
        slot = d - 1

        def body(rows, there):
            value = terms[r](d, part, rows, there)
            if got is not None:
                value = value + got[there, :].astype(F32)
            ring_send[r, slot, rows, :] = value.astype(BF16)
        over_rows(part, body)
        src = ring_send.at[r, slot, pl.ds(part * HALF, HALF)]
        if d == 2:
            push(src, far_in.at[r, part], ring_sems.at[r, part], step_to(r, 1 if part == 0 else 3))
        else:
            side = 0 if d == 1 else 1
            push(src, near_in.at[r, side, part], ring_sems.at[r, 2 + 2 * side + part], step_to(r, d))

    def give_added(r, d):
        part = 0 if d == 1 else 1
        await_all(far_in.at[r, part], ring_sems.at[r, part])
        give(r, d, part, far_in.at[r, part])

    def received(r, part, there):
        return near_in[r, 0, part, there, :].astype(F32) + near_in[r, 1, part, there, :].astype(F32)

    await_weights(2, 0)
    give(0, 2, 0)
    await_weights(2, 1)
    give(0, 2, 1)
    send_weights(1, 0)
    send_weights(3, 1)
    share_grads(0, 1)
    share_grads(0, 3)
    pack_grads(1)
    for k in (2, 1, 3, 0):
        spread_grads(1, k)

    await_all(by_z.at[3], recv_sems.at[9])
    push(by_z.at[3, :CUT], by_z.at[2, :CUT], recv_sems.at[11], at(dzh=1))
    await_all(by_z.at[1], recv_sems.at[10])
    push(by_z.at[1, CUT:], by_z.at[2, CUT:], recv_sems.at[12], at(dzh=3))

    for k in (2, 1, 3, 0):
        share_grads(1, k)
    await_weights(1, 1)
    await_grads(0, 1)
    give(0, 1, 1)
    await_weights(3, 0)
    await_grads(0, 3)
    give(0, 3, 0)
    for i in (0, 1, 3):
        masked(1, i, by_z[i])
    for i in (2, 1, 3, 0):
        await_all(wown.at[i], own_sems.at[i])
    await_grads(1, 2)
    give(1, 2, 0)
    give(1, 2, 1)
    await_grads(1, 1)
    give(1, 1, 1)
    await_grads(1, 3)
    give(1, 3, 0)
    await_all(by_z.at[2, :CUT], recv_sems.at[11])
    await_all(by_z.at[2, CUT:], recv_sems.at[12])
    masked(1, 2, by_z[2])
    give(2, 2, 0)
    give(2, 2, 1)
    give(2, 1, 1)
    give(2, 3, 0)
    await_weights(1, 0)
    give_added(0, 1)
    await_weights(3, 1)
    give_added(0, 3)
    give_added(1, 1)
    give_added(1, 3)
    await_grads(1, 0)
    for part in range(2):
        def hold(rows, there, part=part):
            num_own[rows, :] = own_numerators(0, part, rows, there)
            den_own[rows, :] = denominators(0, part, rows, there)
        over_rows(part, hold)
    give_added(2, 1)
    give_added(2, 3)

    for copy in sends[:-5]:
        copy.wait_send()
    def arrived(r, part):
        for side in range(2):
            await_all(near_in.at[r, side, part], ring_sems.at[r, 2 + 2 * side + part])

    for part in range(2):
        arrived(1, part)
        arrived(2, part)

        def combine(rows, there, part=part):
            num_own[rows, :] = num_own[rows, :] + received(1, part, there)
            den_own[rows, :] = 1.0 / (den_own[rows, :] + received(2, part, there) + epsilon)
        over_rows(part, combine)
    for part in range(2):
        arrived(0, part)

        def finish(rows, there, part=part):
            out_ref[rows, :] = ((num_own[rows, :] + received(0, part, there)) * den_own[rows, :]).astype(BF16)
        over_rows(part, finish)

    for copy in sends[-5:]:
        copy.wait_send()


def per_device(activations, out_grads, owners, weights):
    hbm, vmem = pl.BlockSpec(memory_space=pl.ANY), pl.BlockSpec(memory_space=pltpu.VMEM)
    return pl.pallas_call(
        kernel,
        out_shape=jax.ShapeDtypeStruct((ROWS, COLS), BF16),
        in_specs=[hbm, hbm, pl.BlockSpec(memory_space=pltpu.SMEM), hbm],
        out_specs=vmem,
        scratch_shapes=[
            pltpu.VMEM(activations.shape, BF16),
            pltpu.VMEM(out_grads.shape, BF16),
            pltpu.VMEM((RING, 16, 2 * SIDE), BF16),
            pltpu.VMEM((RING, 16, 2 * SIDE), BF16),
            pltpu.VMEM((2, RING, 16, SIDE), BF16),
            pltpu.VMEM((2, RING, 16, SIDE), BF16),
            pltpu.VMEM((2, RING, 16, COLS), BF16),
            pltpu.VMEM((2, RING, 16, COLS), BF16),
            pltpu.VMEM((2, RING, RING, 16, COLS), BF16),
            pltpu.VMEM((2, RING, 16, WIDE), BF16),
            pltpu.VMEM((2, 2, RING, RING, 16, WIDE), BF16),
            pltpu.VMEM((RING, 16, WIDE), F32),
            pltpu.VMEM((RING, 16, WIDE), F32),
            pltpu.VMEM((SIDE, TOKENS), F32),
            pltpu.VMEM((RING, UNITS, TOKENS), BF16),
            pltpu.VMEM((RING, UNITS, TOKENS), BF16),
            pltpu.VMEM((2, RING, 2, ROWS, TOKENS), BF16),
            pltpu.VMEM((RING - 1, 2, RING, HALF, COLS), BF16),
            pltpu.VMEM((RING, ROWS, COLS), BF16),
            pltpu.VMEM((3, 3, ROWS, COLS), BF16),
            pltpu.VMEM((3, 2, HALF, COLS), BF16),
            pltpu.VMEM((3, 2, 2, HALF, COLS), BF16),
            pltpu.VMEM((ROWS, COLS), F32),
            pltpu.VMEM((ROWS, COLS), F32),
            pltpu.SemaphoreType.DMA((128,)),
            pltpu.SemaphoreType.DMA((14,)),
            pltpu.SemaphoreType.DMA((2 * RING,)),
            pltpu.SemaphoreType.DMA((RING,)),
            pltpu.SemaphoreType.DMA((3, 6)),
            pltpu.SemaphoreType.DMA((2, 2, RING)),
        ],
        compiler_params=pltpu.CompilerParams(
            collective_id=0, has_side_effects=True, vmem_limit_bytes=56 << 20),
    )(activations, out_grads, owners, weights)


def solution(mesh):
    return jax.shard_map(
        per_device,
        mesh=mesh,
        in_specs=(
            P("mp", "shard", None),
            P("mp", "shard", None),
            P("mp", "shard"),
            P("mp", "shard", None),
        ),
        out_specs=P("shard", "mp"),
        check_vma=False,
    )
```

```python
import jax
import jax.numpy as jnp
from jax import lax
from jax.experimental import pallas as pl
from jax.experimental.pallas import tpu as pltpu
from jax.sharding import PartitionSpec as P

MESH = pl.DeviceIdType.MESH
F32, BF16 = jnp.float32, jnp.bfloat16
RING = 4
TOK = 4
TOKENS = 128
ROWS = 448
HALF = ROWS // 2
COLS = 256
WIDE = RING * COLS
PAIR = 2 * ROWS
SIDE = 512
UNITS = ROWS + 16
CUT = 240
TILE = 112
epsilon = 1e-6


def kernel(act_ref, grad_ref, own_ref, w_ref, out_ref,
           act_msg, act_in, act_pack, act_all,
           grad_msg, grad_step, grad_in, grad_pack, grad_all,
           tmp_a, tmp_b, turned, by_y, by_z, lhs, wbuf, wown,
           ring_send, far_in, near_in, num_own, den_own,
           send_sems, recv_sems, w_sems, own_sems, ring_sems, grad_sems):
    mp, shard = lax.axis_index("mp"), lax.axis_index("shard")
    y, zh = mp // RING, lax.rem(mp, RING)
    x, zl, c = shard // (2 * RING), lax.rem(shard // 2, RING), lax.rem(shard, 2)

    def at(dy=0, dzh=0, dx=0, dzl=0, dc=0):
        yy, zz = lax.rem(y + dy, RING), lax.rem(zh + dzh, RING)
        xx, ll = lax.rem(x + dx, RING), lax.rem(zl + dzl, RING)
        cc = lax.rem(c + dc, 2)
        return (yy * RING + zz, (xx * RING + ll) * 2 + cc)

    partners = [at(dy=i) for i in range(1, RING)] + [at(dzl=i) for i in range(1, RING)]
    partners += [at(dzh=i) for i in range(1, RING)]
    partners += [at(dx=i, dc=j) for i in range(RING) for j in range(2) if (i, j) != (0, 0)]

    sends = []

    def push(src, dst, recv_sem, target):
        copy = pltpu.make_async_remote_copy(
            src_ref=src, dst_ref=dst, send_sem=send_sems.at[len(sends)],
            recv_sem=recv_sem, device_id=target, device_id_type=MESH)
        copy.start()
        sends.append(copy)

    def keep(src, dst, sem):
        pltpu.make_async_copy(src, dst, sem).start()

    def await_all(buf, sem):
        pltpu.make_async_copy(buf, buf, sem).wait()

    barrier = pltpu.get_barrier_semaphore()
    for target in partners:
        pl.semaphore_signal(barrier, inc=1, device_id=target, device_id_type=MESH)

    rows4 = lax.broadcasted_iota(jnp.int32, (TOK, 128), 0)
    low = lax.broadcasted_iota(jnp.int32, (TOK, 128), 1) < 64
    owner = jnp.zeros((TOK, 128), F32)
    for t in range(TOK):
        owner = owner + jnp.where(rows4 == t, own_ref[0, t].astype(F32), 0.0)
    for l in range(RING):
        for i in range(RING):
            col = (i * RING + l) * PAIR
            to = slice(TOK * i, TOK * (i + 1))
            middle = act_ref[0, :, col + 384:col + 512].astype(F32)
            tmp_a[l, to, 0:384] = act_ref[0, :, col:col + 384].astype(F32)
            tmp_a[l, to, 384:512] = jnp.where(low, middle, owner)
            tmp_a[l, to, 512:640] = jnp.where(low, owner, middle)
            tmp_a[l, to, 640:1024] = act_ref[0, :, col + 512:col + PAIR].astype(F32)
        act_msg[l] = tmp_a[l].astype(BF16)
    pl.semaphore_wait(barrier, len(partners))

    def send_grads(g):
        ring = zh if g else y
        for i in range(RING):
            src, dst = grad_msg.at[g, lax.rem(ring + i, RING)], grad_step.at[g, ring]
            if i == 0:
                keep(src, dst, recv_sems.at[6 + g])
            else:
                push(src, dst, recv_sems.at[6 + g], at(dzh=i) if g else at(dy=i))

    def send_grads_on(g):
        await_all(grad_step.at[g], recv_sems.at[6 + g])
        for j in range(RING):
            src, dst = grad_step.at[g], grad_in.at[g, :, zl]
            if j == 0:
                keep(src, dst, recv_sems.at[1 + g])
            else:
                push(src, dst, recv_sems.at[1 + g], at(dzl=j))

    def send_weights(d, part):
        slot, rows = d % RING, pl.ds(part * HALF, HALF)
        block = lax.rem(zh + slot, RING)
        for i in (2, 1, 3, 0):
            to = lax.rem(y + i, RING)
            cols = pl.ds(pl.multiple_of(to * WIDE + block * COLS, COLS), COLS)
            src, dst = w_ref.at[0, rows, cols], wbuf.at[slot - 1, part, y]
            if i == 0:
                keep(src, dst, w_sems.at[2 * slot + part])
            else:
                push(src, dst, w_sems.at[2 * slot + part], at(dy=i))

    def await_weights(d, part):
        await_all(wbuf.at[d - 1, part], w_sems.at[2 * d + part])

    for j in range(RING):
        src, dst = act_msg.at[lax.rem(zl + j, RING)], act_in.at[zl]
        if j == 0:
            keep(src, dst, recv_sems.at[0])
        else:
            push(src, dst, recv_sems.at[0], at(dzl=j))
    for g in range(2):
        for i in range(RING):
            for q in range(RING):
                col = i * WIDE + q * COLS if g == 0 else q * WIDE + i * COLS
                tmp_b[i, TOK * q:TOK * (q + 1), :COLS] = grad_ref[0, :, col:col + COLS].astype(F32)
            grad_msg[g, i] = tmp_b[i, :, :COLS].astype(BF16)
    send_grads(0)
    send_grads(1)
    send_weights(2, 0)
    send_weights(2, 1)

    await_all(act_in, recv_sems.at[0])
    for l in range(RING):
        tmp_a[l] = act_in[l].astype(F32)
    for i in range(RING):
        for l in range(RING):
            tmp_b[i, TOK * l:TOK * (l + 1), :] = tmp_a[l, TOK * i:TOK * (i + 1), :]
        for j in range(2):
            act_pack[j, i] = tmp_b[i, :, j * SIDE:(j + 1) * SIDE].astype(BF16)
    for i in range(RING):
        for j in range(2):
            src, dst = act_pack.at[lax.rem(c + j, 2), lax.rem(x + i, RING)], act_all.at[c, x]
            if (i, j) == (0, 0):
                keep(src, dst, recv_sems.at[3])
            else:
                push(src, dst, recv_sems.at[3], at(dx=i, dc=j))
    send_grads_on(0)

    def pack_grads(g):
        await_all(grad_in.at[g], recv_sems.at[1 + g])
        for i in range(RING):
            for l in range(RING):
                tmp_a[l, :, :COLS] = grad_in[g, i, l].astype(F32)
            for l in range(RING):
                for q in range(RING):
                    tmp_b[i, TOK * l:TOK * (l + 1), COLS * q:COLS * (q + 1)] = tmp_a[l, TOK * q:TOK * (q + 1), :COLS]
            grad_pack[g, i] = tmp_b[i].astype(BF16)

    def grad_block(g, k):
        return pl.ds(pl.multiple_of(lax.rem((y if g else zh) + k, RING) * COLS, COLS), COLS)

    def spread_grads(g, k):
        src = grad_pack.at[g, :, :, grad_block(g, k)]
        dst = grad_all.at[g, c, x, :, :, grad_block(g, k)]
        keep(src, dst, grad_sems.at[g, 0, k])
        for i in (2, 1, 3):
            push(src, dst, grad_sems.at[g, 0, k], at(dx=i))

    def share_grads(g, k):
        both = grad_all.at[g, c, :, :, :, grad_block(g, k)]
        await_all(both, grad_sems.at[g, 0, k])
        push(both, both, grad_sems.at[g, 1, k], at(dc=1))

    def await_grads(g, k):
        await_all(grad_all.at[g, 1 - c, :, :, :, grad_block(g, k)], grad_sems.at[g, 1, k])

    await_all(act_all, recv_sems.at[3])
    turned[...] = act_all[...].reshape(TOKENS, SIDE).astype(F32).T
    by_z[0, :ROWS] = turned[pl.ds(pl.multiple_of(c * 64, 64), ROWS), :].astype(BF16)
    by_z[0, ROWS:] = turned[pl.ds(pl.multiple_of((1 - c) * ROWS, 64), 16), :].astype(BF16)
    push(by_z.at[0], by_z.at[3], recv_sems.at[9], at(dzh=1))
    push(by_z.at[0], by_z.at[1], recv_sems.at[10], at(dzh=3))
    for i in (2, 1, 3):
        push(by_z.at[0], by_y.at[y], recv_sems.at[8], at(dy=i))
    keep(by_z.at[0], by_y.at[y], recv_sems.at[8])
    pack_grads(0)
    for k in (2, 1, 3):
        spread_grads(0, k)
    send_grads_on(1)
    for i in (2, 1, 3, 0):
        cols = lax.rem(y + i, RING) * WIDE + zh * COLS
        keep(w_ref.at[0, :, pl.ds(pl.multiple_of(cols, COLS), COLS)], wown.at[i], own_sems.at[i])

    def masked(g, i, units):
        one = units[ROWS:]
        body = units[:ROWS].reshape(ROWS // 16, 16, TOKENS)
        lhs[g, i, 0] = (body * (1 - one)[None]).reshape(ROWS, TOKENS)
        lhs[g, i, 1] = (body * one[None]).reshape(ROWS, TOKENS)

    share_grads(0, 2)
    await_all(by_y, recv_sems.at[8])
    send_weights(1, 1)
    send_weights(3, 0)
    for i in range(RING):
        masked(0, i, by_y[i])
    await_grads(0, 2)

    def fishers(g, block, rows, models=RING):
        cols = pl.ds(pl.multiple_of(block * COLS, COLS), COLS)
        for i in range(models):
            model = i if g == 0 else lax.rem(zh + i, RING)
            grads = grad_all[g, :, :, model, :, cols].reshape(TOKENS, COLS)
            one = jnp.dot(lhs[g, i, 0, rows, :], grads, preferred_element_type=F32)
            two = jnp.dot(lhs[g, i, 1, rows, :], grads, preferred_element_type=F32)
            yield ((one * one + two * two) * 0.5).astype(BF16).astype(F32)

    def over_rows(part, body):
        @pl.loop(0, HALF // TILE, unroll=1)
        def _(step):
            there = pl.ds(pl.multiple_of(step * TILE, TILE), TILE)
            rows = pl.ds(pl.multiple_of(part * HALF + step * TILE, TILE), TILE)
            body(rows, there)

    def y_ring_numerators(d, part, rows, there):
        num = jnp.zeros((TILE, COLS), F32)
        for i, fisher in enumerate(fishers(0, lax.rem(zh + d, RING), rows)):
            num = num + fisher * wbuf[d - 1, part, i, there, :].astype(F32)
        return num

    def own_numerators(d, part, rows, there):
        for fisher in fishers(1, lax.rem(y + d, RING), rows, 1):
            return fisher * wown[d, rows, :].astype(F32)

    def denominators(d, part, rows, there):
        den = jnp.zeros((TILE, COLS), F32)
        for fisher in fishers(1, lax.rem(y + d, RING), rows):
            den = den + fisher
        return den

    terms = (y_ring_numerators, own_numerators, denominators)

    def step_to(r, d):
        return at(dzh=d) if r == 0 else at(dy=d)

    def give(r, d, part, got=None):
        slot = d - 1

        def body(rows, there):
            value = terms[r](d, part, rows, there)
            if got is not None:
                value = value + got[there, :].astype(F32)
            ring_send[r, slot, rows, :] = value.astype(BF16)
        over_rows(part, body)
        src = ring_send.at[r, slot, pl.ds(part * HALF, HALF)]
        if d == 2:
            push(src, far_in.at[r, part], ring_sems.at[r, part], step_to(r, 1 if part == 0 else 3))
        else:
            side = 0 if d == 1 else 1
            push(src, near_in.at[r, side, part], ring_sems.at[r, 2 + 2 * side + part], step_to(r, d))

    def give_added(r, d):
        part = 0 if d == 1 else 1
        await_all(far_in.at[r, part], ring_sems.at[r, part])
        give(r, d, part, far_in.at[r, part])

    def received(r, part, there):
        return near_in[r, 0, part, there, :].astype(F32) + near_in[r, 1, part, there, :].astype(F32)

    await_weights(2, 0)
    give(0, 2, 0)
    await_weights(2, 1)
    give(0, 2, 1)
    send_weights(1, 0)
    send_weights(3, 1)
    share_grads(0, 1)
    share_grads(0, 3)
    pack_grads(1)
    for k in (2, 1, 3, 0):
        spread_grads(1, k)

    await_all(by_z.at[3], recv_sems.at[9])
    push(by_z.at[3, :CUT], by_z.at[2, :CUT], recv_sems.at[11], at(dzh=1))
    await_all(by_z.at[1], recv_sems.at[10])
    push(by_z.at[1, CUT:], by_z.at[2, CUT:], recv_sems.at[12], at(dzh=3))

    for k in (2, 1, 3, 0):
        share_grads(1, k)
    await_weights(1, 1)
    await_grads(0, 1)
    give(0, 1, 1)
    await_weights(3, 0)
    await_grads(0, 3)
    give(0, 3, 0)
    for i in (0, 1, 3):
        masked(1, i, by_z[i])
    for i in (2, 1, 3, 0):
        await_all(wown.at[i], own_sems.at[i])
    await_grads(1, 2)
    give(1, 2, 0)
    give(1, 2, 1)
    await_grads(1, 1)
    give(1, 1, 1)
    await_grads(1, 3)
    give(1, 3, 0)
    await_all(by_z.at[2, :CUT], recv_sems.at[11])
    await_all(by_z.at[2, CUT:], recv_sems.at[12])
    masked(1, 2, by_z[2])
    give(2, 2, 0)
    give(2, 2, 1)
    give(2, 1, 1)
    give(2, 3, 0)
    await_weights(1, 0)
    give_added(0, 1)
    await_weights(3, 1)
    give_added(0, 3)
    give_added(1, 1)
    give_added(1, 3)
    await_grads(1, 0)
    for part in range(2):
        def hold(rows, there, part=part):
            num_own[rows, :] = own_numerators(0, part, rows, there)
            den_own[rows, :] = denominators(0, part, rows, there)
        over_rows(part, hold)
    give_added(2, 1)
    give_added(2, 3)

    for copy in sends[:-6]:
        copy.wait_send()
    def arrived(r, part):
        for side in range(2):
            await_all(near_in.at[r, side, part], ring_sems.at[r, 2 + 2 * side + part])

    for part in range(2):
        arrived(1, part)
        arrived(2, part)

        def combine(rows, there, part=part):
            num_own[rows, :] = num_own[rows, :] + received(1, part, there)
            den_own[rows, :] = 1.0 / (den_own[rows, :] + received(2, part, there) + epsilon)
        over_rows(part, combine)
    for part in range(2):
        arrived(0, part)

        def finish(rows, there, part=part):
            out_ref[rows, :] = ((num_own[rows, :] + received(0, part, there)) * den_own[rows, :]).astype(BF16)
        over_rows(part, finish)

    for copy in sends[-6:]:
        copy.wait_send()


def per_device(activations, out_grads, owners, weights):
    hbm, vmem = pl.BlockSpec(memory_space=pl.ANY), pl.BlockSpec(memory_space=pltpu.VMEM)
    return pl.pallas_call(
        kernel,
        out_shape=jax.ShapeDtypeStruct((ROWS, COLS), BF16),
        in_specs=[vmem, vmem, pl.BlockSpec(memory_space=pltpu.SMEM), hbm],
        out_specs=vmem,
        scratch_shapes=[
            pltpu.VMEM((RING, 16, 2 * SIDE), BF16),
            pltpu.VMEM((RING, 16, 2 * SIDE), BF16),
            pltpu.VMEM((2, RING, 16, SIDE), BF16),
            pltpu.VMEM((2, RING, 16, SIDE), BF16),
            pltpu.VMEM((2, RING, 16, COLS), BF16),
            pltpu.VMEM((2, RING, 16, COLS), BF16),
            pltpu.VMEM((2, RING, RING, 16, COLS), BF16),
            pltpu.VMEM((2, RING, 16, WIDE), BF16),
            pltpu.VMEM((2, 2, RING, RING, 16, WIDE), BF16),
            pltpu.VMEM((RING, 16, WIDE), F32),
            pltpu.VMEM((RING, 16, WIDE), F32),
            pltpu.VMEM((SIDE, TOKENS), F32),
            pltpu.VMEM((RING, UNITS, TOKENS), BF16),
            pltpu.VMEM((RING, UNITS, TOKENS), BF16),
            pltpu.VMEM((2, RING, 2, ROWS, TOKENS), BF16),
            pltpu.VMEM((RING - 1, 2, RING, HALF, COLS), BF16),
            pltpu.VMEM((RING, ROWS, COLS), BF16),
            pltpu.VMEM((3, 3, ROWS, COLS), BF16),
            pltpu.VMEM((3, 2, HALF, COLS), BF16),
            pltpu.VMEM((3, 2, 2, HALF, COLS), BF16),
            pltpu.VMEM((ROWS, COLS), F32),
            pltpu.VMEM((ROWS, COLS), F32),
            pltpu.SemaphoreType.DMA((128,)),
            pltpu.SemaphoreType.DMA((14,)),
            pltpu.SemaphoreType.DMA((2 * RING,)),
            pltpu.SemaphoreType.DMA((RING,)),
            pltpu.SemaphoreType.DMA((3, 6)),
            pltpu.SemaphoreType.DMA((2, 2, RING)),
        ],
        compiler_params=pltpu.CompilerParams(
            collective_id=0, has_side_effects=True, vmem_limit_bytes=56 << 20),
    )(activations, out_grads, owners, weights)


def solution(mesh):
    return jax.shard_map(
        per_device,
        mesh=mesh,
        in_specs=(
            P("mp", "shard", None),
            P("mp", "shard", None),
            P("mp", "shard"),
            P("mp", "shard", None),
        ),
        out_specs=P("shard", "mp"),
        check_vma=False,
    )
```
